32 devices in a mesh: dom: 4 (over x, core), mem: 8 (over z, y).
Axes of the slice: x: 2, y: 2, z: 4, core: 2. Of those that a mesh axis runs over, the one named last changes fastest.
Arguments:
- state: float32 [1024, 32768], P('mem', 'dom'), may hold values from -14 to 14, as said below
- obs_ensemble: float32 [1024, 2048], P('mem', 'dom'), may hold values from -14 to 14, as said below
- innovations: float32 [1024, 2048], P('mem', 'dom'), may hold values from -6 to 6
- obs_coords: float32 [2, 2048], P(None, 'dom'), may hold values from 0 to 4, as said below
- tile_list: int32 [4, 8, 2, 48], P('dom', 'mem'), may hold values from 0 to 11, as said below
- tile_counts: int32 [4, 8], P('dom', 'mem'), may hold values from 24 to 48, as said below
Outputs:
- analysis: float32 [1024, 32768], P(None, ('dom', 'mem'))
The draws below stay inside these ranges and needn't reach their ends.
Inputs may be any that keep to these rules, and one draw needn't show every extreme that they name: `state`: forecast values of each gridpoint: an offset plus a spread of its own times a bounded noise. `obs_ensemble`: Observation-space values of each observation: an offset plus a spread of its own times a bounded noise. `obs_coords`: the observations of domain d have a first coordinate within [d, d + 1) and a second within [0, 1). `tile_list`: slots k * 6 to (k + 1) * 6 - 1 name point block k (of 8) and 6 distinct observation blocks of the window of 12 blocks: the left neighbour domain's, the own domain's, the right neighbour domain's, domains on a cycle. `tile_counts`: slots below the count are live. Some group has all 48 live, some other group half of them.
All inputs are finite; a program needn't handle non-finite values.
Results may differ from the reference program's by a relative error of at most 0.0002.
Values sent between devices are 32-bit elements; how exact they have to be, the bound alone decides.
No kernel may reach another device: no remote copies, remote signals or barrier semaphores. Data moves between devices by JAX's collectives and lax.ppermute only.
A program may use at most 192 MiB of HBM per device.

```python
import jax
import jax.numpy as jnp
from jax import lax

M = 1024
BLK = 128
PTS_DEV = 1024
OBS_DOM = 512
TPB = 6
DOMAINS = 4
GROUPS = 8
PTS_DOM = 8192
PTS = 32768
OBS = 2048
TILES = 48


def draw_spread(key, rows, columns):
    key_offset, key_scale, key_noise = jax.random.split(key, 3)
    offset = jax.random.uniform(key_offset, (1, columns), jnp.float32, -2.0, 2.0)
    scale = jnp.exp(jax.random.uniform(key_scale, (1, columns), jnp.float32, jnp.log(0.3), jnp.log(3.0)))
    noise = jax.random.truncated_normal(key_noise, -4.0, 4.0, (rows, columns), jnp.float32)
    return offset + scale * noise


def draw_state(key, part):
    return draw_spread(jax.random.fold_in(key, 11), M, PTS)


def draw_obs_ensemble(key, part):
    return draw_spread(jax.random.fold_in(key, 23), M, OBS)


def draw_obs_coords(key, part):
    key_x, key_y = jax.random.split(jax.random.fold_in(key, 37))
    domain = (jnp.arange(OBS) // OBS_DOM).astype(jnp.float32)
    along = jax.random.uniform(key_x, (OBS,), jnp.float32, 0.0, 0.999)
    across = jax.random.uniform(key_y, (OBS,), jnp.float32, 0.0, 1.0)
    return jnp.stack([domain + along, across], axis=0)


def block_order(subkey):
    return jax.random.permutation(subkey, 3 * (OBS_DOM // BLK))[:TPB]


def draw_tile_list(key, part):
    nblocks = PTS_DEV // BLK
    subkeys = jax.random.split(jax.random.fold_in(key, 41), DOMAINS * GROUPS * nblocks)
    orders = jax.vmap(block_order)(subkeys)
    obs_part = orders.reshape(DOMAINS, GROUPS, nblocks * TPB).astype(jnp.int32)
    point_part = jnp.broadcast_to((jnp.arange(nblocks * TPB, dtype=jnp.int32) // TPB)[None, None, :], (DOMAINS, GROUPS, nblocks * TPB))
    return jnp.stack([point_part, obs_part], axis=2).astype(jnp.int32)


def draw_tile_counts(key, part):
    key_count, key_pick = jax.random.split(jax.random.fold_in(key, 53))
    total = DOMAINS * GROUPS
    counts = jax.random.randint(key_count, (total,), TILES // 2, TILES + 1)
    chosen = jax.random.randint(key_pick, (), 0, total)
    counts = counts.at[chosen].set(TILES)
    counts = counts.at[(chosen + 1) % total].set(TILES // 2)
    return counts.reshape(DOMAINS, GROUPS).astype(jnp.int32)


def shard_levels(own_key, extent, cuts, least, top_value):
    factor_of = 1.0
    for dim, parts in cuts:
        heights = jax.random.uniform(jax.random.fold_in(jax.random.fold_in(own_key, 6), dim), (parts,), jnp.float32, least / len(cuts), top_value / len(cuts))
        factor_of = factor_of * jnp.repeat(jnp.exp(heights), extent[dim] // parts).reshape((-1,) + (1,) * (len(extent) - 1 - dim))
    return factor_of


def centred(key, extent, scale, reach, cuts=(), kind=jnp.bfloat16):
    array = jax.random.normal(key, extent, jnp.float32) * scale
    if len(cuts) > 0:
        array = shard_levels(key, extent, cuts, -0.22, 0.18) * array
    return jnp.clip(array, min=-reach, max=reach).astype(kind)


def setup_inputs(seed: int = 0) -> dict:
    key_of = jax.random.split(jax.random.key(seed), 7)
    return {
        "state": draw_state(jax.random.fold_in(key_of[6], 71), 0),
        "obs_ensemble": draw_obs_ensemble(jax.random.fold_in(key_of[6], 71), 0),
        "innovations": centred(key_of[2], (M, OBS), 1.0, 6.0, ((0, 8), (1, 4)), jnp.float32),
        "obs_coords": draw_obs_coords(jax.random.fold_in(key_of[6], 71), 0),
        "tile_list": draw_tile_list(jax.random.fold_in(key_of[6], 71), 0),
        "tile_counts": draw_tile_counts(jax.random.fold_in(key_of[6], 71), 0),
    }


taper_reach = 0.6


def taper_of(point_x, point_y, obs_x, obs_y, cycle_size):
    gap_x = jnp.abs(point_x[:, :, None] - obs_x[:, None, :])
    gap_x = jnp.minimum(gap_x, cycle_size - gap_x)
    gap_y = point_y[:, :, None] - obs_y[:, None, :]
    return jnp.exp(-(gap_x * gap_x + gap_y * gap_y) / (2.0 * taper_reach * taper_reach))


def reference(state, obs_ensemble, innovations, obs_coords, tile_list, tile_counts):
    anomalies = obs_ensemble - jnp.mean(obs_ensemble, axis=0, keepdims=True)
    obs_blocks = OBS_DOM // BLK
    cycle_size = float(DOMAINS)
    row_count = float(PTS_DOM // 32)

    def one_device(device, output):
        device = jnp.asarray(device).astype(jnp.int32)
        domain = device // GROUPS
        group_id = device % GROUPS
        start = (domain * PTS_DOM + group_id * PTS_DEV).astype(jnp.int32)
        live_count = tile_counts[domain, group_id]

        def one_tile(slot_index, change):
            slot_index = jnp.asarray(slot_index).astype(jnp.int32)
            pblock = tile_list[domain, group_id, 0, slot_index]
            oblock = tile_list[domain, group_id, 1, slot_index]
            src_domain = (domain - 1 + oblock // obs_blocks + DOMAINS) % DOMAINS
            column = (src_domain * OBS_DOM + (oblock % obs_blocks) * BLK).astype(jnp.int32)
            offset = (pblock * BLK).astype(jnp.int32)
            x_block = lax.dynamic_slice_in_dim(state, start + offset, BLK, 1)
            y_block = lax.dynamic_slice_in_dim(anomalies, column, BLK, 1)
            w_block = lax.dynamic_slice_in_dim(innovations, column, BLK, 1)
            c_block = lax.dynamic_slice_in_dim(obs_coords, column, BLK, 1)
            covariance = jnp.dot(x_block.T, y_block, precision=lax.Precision.HIGHEST) / (M - 1)
            within = group_id * PTS_DEV + pblock * BLK + jnp.arange(BLK, dtype=jnp.int32)
            point_x = domain.astype(jnp.float32) + ((within % 32).astype(jnp.float32) + 0.5) / 32.0
            point_y = ((within // 32).astype(jnp.float32) + 0.5) / row_count
            taper = taper_of(point_x[None], point_y[None], c_block[0][None], c_block[1][None], cycle_size)[0]
            live_mask = (slot_index < live_count).astype(jnp.float32)
            weights = taper * covariance * live_mask
            increment = jnp.dot(w_block, weights.T, precision=lax.Precision.HIGHEST)
            before = lax.dynamic_slice_in_dim(change, offset, BLK, 1)
            return lax.dynamic_update_slice_in_dim(change, before + increment, offset, 1)

        change = lax.fori_loop(0, TILES, one_tile, jnp.zeros((M, PTS_DEV), jnp.float32))
        updated = lax.dynamic_slice_in_dim(state, start, PTS_DEV, 1) + change
        return lax.dynamic_update_slice_in_dim(output, updated, start, 1)

    return lax.fori_loop(0, DOMAINS * GROUPS, one_device, state)
```

```python
import functools

import jax
import jax.numpy as jnp
from jax import lax
from jax.experimental import pallas as pl
from jax.experimental.pallas import tpu as pltpu
from jax.sharding import PartitionSpec as P

taper_reach = 0.6
tile_side = 128
chunks = 2
pieces = 2
f32, bf16 = jnp.float32, jnp.bfloat16
anywhere = pl.BlockSpec(memory_space=pl.ANY)
in_vmem = pl.BlockSpec(memory_space=pltpu.VMEM)
vmem_limit = 56 * 1024 * 1024


def dot(a, b):
    return lax.dot_general(a, b, (((1,), (0,)), ((), ())), preferred_element_type=f32)


def split(x):
    high = x.astype(bf16)
    return high, (x - high.astype(f32)).astype(bf16)


def swap(x, axis, distance):
    size = lax.axis_size(axis)
    return lax.ppermute(x, axis, [(i, i ^ distance) for i in range(size)])


def prep_obs_kernel(order, x_ref, high_ref, low_ref):
    blocks, rows, _ = x_ref.shape
    total = jnp.sum(x_ref[0], axis=0, keepdims=True)
    for i in range(1, blocks):
        total += jnp.sum(x_ref[i], axis=0, keepdims=True)
    mean = total / (blocks * rows)
    for i in range(blocks):
        high, low = split((x_ref[i] - mean).T)
        at = pl.ds(order[i] * rows, rows)
        high_ref[:, at] = high
        low_ref[:, at] = low


def prep_obs(x, order):
    blocks, rows, width = x.shape
    return pl.pallas_call(
        functools.partial(prep_obs_kernel, order),
        out_shape=[jax.ShapeDtypeStruct((width, blocks * rows), bf16)] * 2,
        in_specs=[in_vmem],
        out_specs=[in_vmem] * 2,
        compiler_params=pltpu.CompilerParams(vmem_limit_bytes=vmem_limit),
        cost_estimate=pl.CostEstimate(flops=8 * x.size, bytes_accessed=8 * x.size, transcendentals=0),
    )(x)


def prep_innov_kernel(order, x_ref, high_ref, low_ref):
    blocks, rows, _ = x_ref.shape
    for i in range(blocks):
        high, low = split(x_ref[i])
        at = pl.ds(order[i] * rows, rows)
        high_ref[at, :] = high
        low_ref[at, :] = low


def prep_innov(x, order):
    blocks, rows, width = x.shape
    return pl.pallas_call(
        functools.partial(prep_innov_kernel, order),
        out_shape=[jax.ShapeDtypeStruct((blocks * rows, width), bf16)] * 2,
        in_specs=[in_vmem],
        out_specs=[in_vmem] * 2,
        compiler_params=pltpu.CompilerParams(vmem_limit_bytes=vmem_limit),
        cost_estimate=pl.CostEstimate(flops=4 * x.size, bytes_accessed=8 * x.size, transcendentals=0),
    )(x)


def update_kernel(npoint, nobs, first, start, *refs):
    me_ref = refs[0]
    refs = refs[1:]
    points, refs = refs[:npoint], refs[npoint:]
    obs_high, refs = refs[:nobs], refs[nobs:]
    obs_low, refs = refs[:nobs], refs[nobs:]
    inn_high, refs = refs[:nobs], refs[nobs:]
    inn_low, refs = refs[:nobs], refs[nobs:]
    taper = refs[0]
    refs = refs[1 if first else 2 :]
    out, total, x_high, x_low, yh, yl, wh, wl, tap, sem_x, sem_y, sem_out = refs
    rows = points[0].shape[0]
    width = points[0].shape[1]
    group = yh.shape[1]
    x_copies = [
        pltpu.make_async_copy(points[i], total.at[pl.ds(i * rows, rows)], sem_x.at[i])
        for i in range(npoint)
    ]
    obs_copies = []
    for i in range(nobs):
        obs_copies.append(
            [
                pltpu.make_async_copy(obs_high[i], yh.at[i], sem_y.at[i, 0]),
                pltpu.make_async_copy(obs_low[i], yl.at[i], sem_y.at[i, 1]),
                pltpu.make_async_copy(
                    taper.at[pl.ds(i * group, group), pl.ds(start, width)], tap.at[i], sem_y.at[i, 2]
                ),
                pltpu.make_async_copy(inn_high[i], wh.at[i], sem_y.at[i, 3]),
                pltpu.make_async_copy(inn_low[i], wl.at[i], sem_y.at[i, 4]),
            ]
        )
    for copy in x_copies:
        copy.start()
    for group_copies in obs_copies:
        for copy in group_copies:
            copy.start()
    for i, copy in enumerate(x_copies):
        copy.wait()
        at = pl.ds(i * rows, rows)
        x_high[at, :], x_low[at, :] = split(total[at, :])

    for i in range(nobs):
        for copy in obs_copies[i][:3]:
            copy.wait()
        cov = dot(yh[i], x_high[...]) + dot(yl[i], x_high[...]) + dot(yh[i], x_low[...])
        weight_high, weight_low = split(cov * tap[i])
        for copy in obs_copies[i][3:]:
            copy.wait()
        total[...] += (
            dot(wh[i], weight_high) + dot(wl[i], weight_high) + dot(wh[i], weight_low)
        )
    me = me_ref[0]
    local = sem_out.shape[0]
    members = total.shape[0]
    ml = members // local
    out_copies = [
        pltpu.make_async_copy(
            total.at[pl.ds(r * ml, ml)],
            out.at[pl.ds(pl.multiple_of((me ^ r) * ml, 8), ml), pl.ds(start, width)],
            sem_out.at[r],
        )
        for r in range(local)
    ]
    for copy in out_copies:
        copy.start()
    for copy in out_copies:
        copy.wait()


def update(me, blocks, obs, innov, taper, out, start, groups, per_device):
    npoint, nobs = len(blocks), len(obs)
    rows, width = blocks[0].shape
    members = rows * npoint
    group = obs[0][0].shape[0]
    first = out is None
    operands = [me, *blocks]
    operands += [o[0] for o in obs] + [o[1] for o in obs]
    operands += [w[0] for w in innov] + [w[1] for w in innov]
    operands += [taper] + ([] if first else [out])
    flops = 3 * 4 * members * width * group * nobs
    return pl.pallas_call(
        functools.partial(update_kernel, npoint, nobs, first, start),
        out_shape=jax.ShapeDtypeStruct((members, per_device), f32),
        in_specs=[pl.BlockSpec(memory_space=pltpu.SMEM)] + [anywhere] * (len(operands) - 1),
        out_specs=anywhere,
        scratch_shapes=[
            pltpu.VMEM((members, width), f32),
            pltpu.VMEM((members, width), bf16),
            pltpu.VMEM((members, width), bf16),
            pltpu.VMEM((nobs, group, members), bf16),
            pltpu.VMEM((nobs, group, members), bf16),
            pltpu.VMEM((nobs, members, group), bf16),
            pltpu.VMEM((nobs, members, group), bf16),
            pltpu.VMEM((nobs, group, width), f32),
            pltpu.SemaphoreType.DMA((npoint,)),
            pltpu.SemaphoreType.DMA((nobs, 5)),
            pltpu.SemaphoreType.DMA((groups,)),
        ],
        input_output_aliases={} if first else {len(operands) - 1: 0},
        compiler_params=pltpu.CompilerParams(vmem_limit_bytes=vmem_limit),
        cost_estimate=pl.CostEstimate(
            flops=flops, bytes_accessed=8 * group * nobs * members, transcendentals=0
        ),
    )(*operands)


def shards(state, obs_ensemble, innovations, obs_coords, tile_list, tile_counts):
    ml = state.shape[0]
    groups = lax.axis_size("mem")
    domains = lax.axis_size("dom")
    per_domain = state.shape[1]
    per_device = per_domain // groups
    obs_local = obs_ensemble.shape[1]
    members = ml * groups
    me = lax.axis_index("mem")
    domain = lax.axis_index("dom")
    odd = domain % 2
    side = me % 2
    far = me // 2
    nfar = groups // 2

    bits = []
    b = groups // 2
    while b >= 1:
        bits.append(b)
        b //= 2
    order = [0]
    for b in bits:
        order = order + [r ^ b for r in order]

    def gathered(x):
        x = x[None]
        for b in bits:
            x = jnp.concatenate([x, swap(x, "mem", b)], axis=0)
        return x

    across = [((i + 1) % domains, (i + 2) % domains) for i in range(0, domains, 2)]
    across = across + [(t, s) for s, t in across]
    chip = [(i, i ^ 1) for i in range(domains)]

    width_piece = obs_local // pieces

    def collected(array, prep):
        out = []
        for p in range(pieces):
            own = gathered(array[:, p * width_piece : (p + 1) * width_piece])
            beside = lax.ppermute(own, "dom", chip)
            beyond = lax.ppermute(own, "dom", across)
            out.append([prep(x, order) for x in (own, beside, beyond)])
        return [out[p][s] for s in range(3) for p in range(pieces)]

    obs = collected(obs_ensemble, prep_obs)
    innov = collected(innovations, prep_innov)

    width = per_device // chunks
    grid = state.reshape(ml, nfar, 2, per_device)
    point_blocks = []
    for c in range(chunks):
        part = lax.slice_in_dim(grid, c * width, (c + 1) * width, axis=3)
        keep = lax.dynamic_index_in_dim(part, side, 2, False).transpose(1, 0, 2)
        give = lax.dynamic_index_in_dim(part, 1 - side, 2, False).transpose(1, 0, 2)
        got = swap(give, "mem", 1)
        blocks = []
        for j in range(nfar):
            pair = jnp.concatenate(
                [
                    lax.dynamic_index_in_dim(keep, far ^ j, 0, False),
                    lax.dynamic_index_in_dim(got, far ^ j, 0, False),
                ],
                axis=0,
            )
            blocks.append(pair if j == 0 else swap(pair, "mem", 2 * j))
        point_blocks.append(blocks)

    coord_own = obs_coords
    coord_beside = lax.ppermute(obs_coords, "dom", chip)
    coord_beyond = lax.ppermute(obs_coords, "dom", across)
    coords = jnp.concatenate([coord_own, coord_beside, coord_beyond], axis=1)
    nblocks = per_device // tile_side
    window = obs_local // tile_side
    point_ids, obs_ids = tile_list[0, 0, 0], tile_list[0, 0, 1]
    slots = point_ids.shape[0]
    live = (jnp.arange(slots, dtype=jnp.int32) < tile_counts[0, 0]).astype(f32)
    position = jnp.stack([jnp.int32(1), 2 - 2 * odd, 2 * odd]).astype(jnp.int32)
    block_ids = (position[:, None] * window + jnp.arange(window, dtype=jnp.int32)[None]).reshape(-1)
    by_obs = (obs_ids[None, :] == block_ids[:, None]).astype(f32) * live[None]
    by_point = (point_ids[:, None] == jnp.arange(nblocks, dtype=jnp.int32)[None]).astype(f32)
    mask = jnp.sum(by_obs[:, :, None] * by_point[None], axis=1)
    mask = jnp.repeat(mask, tile_side, axis=1) / (members - 1)
    within = me * per_device + jnp.arange(per_device, dtype=jnp.int32)
    point_x = domain.astype(f32) + ((within % 32).astype(f32) + 0.5) / 32.0
    point_y = ((within // 32).astype(f32) + 0.5) / float(per_domain // 32)
    gap_x = jnp.abs(point_x[None, :] - coords[0][:, None])
    gap_x = jnp.minimum(gap_x, float(domains) - gap_x)
    gap_y = point_y[None, :] - coords[1][:, None]
    taper = jnp.exp(-(gap_x * gap_x + gap_y * gap_y) / (2.0 * taper_reach * taper_reach))
    taper = (taper.reshape(-1, tile_side, per_device) * mask[:, None, :]).reshape(-1, per_device)

    out = None
    for c in range(chunks):
        out = update(
            me.astype(jnp.int32).reshape(1),
            point_blocks[c],
            obs,
            innov,
            taper,
            out,
            c * width,
            groups,
            per_device,
        )
    return out


def solution(mesh):
    return jax.shard_map(
        shards,
        mesh=mesh,
        in_specs=(
            P("mem", "dom"),
            P("mem", "dom"),
            P("mem", "dom"),
            P(None, "dom"),
            P("dom", "mem", None, None),
            P("dom", "mem"),
        ),
        out_specs=P(None, ("dom", "mem")),
        check_vma=False,
    )
```

```python
import functools

import jax
import jax.numpy as jnp
from jax import lax
from jax.experimental import pallas as pl
from jax.experimental.pallas import tpu as pltpu
from jax.sharding import PartitionSpec as P

taper_reach = 0.6
tile_side = 128
f32, bf16 = jnp.float32, jnp.bfloat16
anywhere = pl.BlockSpec(memory_space=pl.ANY)
in_vmem = pl.BlockSpec(memory_space=pltpu.VMEM)
span_edges = (0, 6, 8)
small_cost = pl.CostEstimate(flops=1000, bytes_accessed=1000, transcendentals=0)
vmem_limit = 56 * 1024 * 1024


def dot(a, b):
    return lax.dot_general(a, b, (((1,), (0,)), ((), ())), preferred_element_type=f32)


def split(x):
    high = x.astype(bf16)
    return high, (x - high.astype(f32)).astype(bf16)


def swap(x, axis, distance):
    size = lax.axis_size(axis)
    return lax.ppermute(x, axis, [(i, i ^ distance) for i in range(size)])


def after(x, *deps):
    return lax.optimization_barrier((x, *deps))[0] if deps else x


def join_kernel(a_ref, b_ref, out_ref, sems):
    size = a_ref.shape[0]
    copies = [
        pltpu.make_async_copy(a_ref, out_ref.at[pl.ds(0, size)], sems.at[0]),
        pltpu.make_async_copy(b_ref, out_ref.at[pl.ds(size, size)], sems.at[1]),
    ]
    for copy in copies:
        copy.start()
    for copy in copies:
        copy.wait()


def join(a, b):
    return pl.pallas_call(
        join_kernel,
        out_shape=jax.ShapeDtypeStruct((2 * a.shape[0], *a.shape[1:]), a.dtype),
        in_specs=[anywhere] * 2,
        out_specs=in_vmem,
        scratch_shapes=[pltpu.SemaphoreType.DMA((2,))],
        compiler_params=pltpu.CompilerParams(vmem_limit_bytes=vmem_limit),
        cost_estimate=small_cost,
    )(a, b)


def prep_obs_kernel(order, near_ref, far_ref, high_ref, low_ref):
    blocks, rows, width = near_ref.shape
    refs = [near_ref.at[i] for i in range(blocks)] + [far_ref.at[i] for i in range(blocks)]
    total = jnp.zeros((1, width), f32)
    for ref in refs:
        total += jnp.sum(ref[...], axis=0, keepdims=True)
    mean = total / (2 * blocks * rows)
    for i, ref in enumerate(refs):
        high, low = split((ref[...] - mean).T)
        at = pl.ds(order[i] * rows, rows)
        high_ref[:, at] = high
        low_ref[:, at] = low


def prep_obs(pair, order):
    blocks, rows, width = pair[0].shape
    whole = pl.BlockSpec((blocks, rows, 128), lambda j: (0, 0, j))
    return pl.pallas_call(
        functools.partial(prep_obs_kernel, order),
        grid=(width // 128,),
        out_shape=[jax.ShapeDtypeStruct((width, 2 * blocks * rows), bf16)] * 2,
        in_specs=[whole] * 2,
        out_specs=[pl.BlockSpec((128, 2 * blocks * rows), lambda j: (j, 0))] * 2,
        compiler_params=pltpu.CompilerParams(vmem_limit_bytes=vmem_limit),
        cost_estimate=small_cost,
    )(*pair)


def update_kernel(parts, order, first, start, *refs):
    me_ref, points, refs = refs[0], refs[1], refs[2:]
    me = me_ref[0]
    nobs = len(parts)
    obs_high, refs = refs[:nobs], refs[nobs:]
    obs_low, refs = refs[:nobs], refs[nobs:]
    ninn = len(refs) - (15 if first else 16)
    inn, refs = refs[:ninn], refs[ninn:]
    taper = refs[0]
    refs = refs[1 if first else 2 :]
    out, total, x_high, x_low, yh, yl, w, tap, kh, kl, sem_x, sem_y, sem_w, sem_out = refs
    members, width = total.shape
    local = len(order)
    ml = members // local
    window = tap.shape[0]
    slot_obs = window // 3
    band = min(512, members)
    x_copies = [
        pltpu.make_async_copy(
            points.at[lax.div(me ^ r, 2), r % 2], total.at[pl.ds(r * ml, ml)], sem_x
        )
        for r in range(local)
    ]
    y_copies = []
    for i, (slot, at, size) in enumerate(parts):
        here = pl.ds(at, size)
        y_copies.append(
            [
                pltpu.make_async_copy(obs_high[i], yh.at[here], sem_y.at[slot, 0]),
                pltpu.make_async_copy(obs_low[i], yl.at[here], sem_y.at[slot, 1]),
                pltpu.make_async_copy(
                    taper.at[here, pl.ds(start, width)], tap.at[here], sem_y.at[slot, 2]
                ),
            ]
        )
    w_copies = []
    for i in range(ninn):
        slot, part = i // 2, i % 2
        here = pl.ds(slot * slot_obs, slot_obs)
        for k in range(local // 2):
            at = pl.ds(order[part * (local // 2) + k] * ml, ml)
            w_copies.append(pltpu.make_async_copy(inn[i].at[k], w.at[at, here], sem_w))
    for copy in x_copies + y_copies[0]:
        copy.start()
    pltpu.make_async_copy(total, total, sem_x).wait()

    def halves(i, carry):
        at = pl.ds(pl.multiple_of(i * 128, 128), 128)
        x_high[at, :], x_low[at, :] = split(total[at, :])
        return carry

    lax.fori_loop(0, members // 128, halves, 0)
    for copy in y_copies[1] + y_copies[2] + w_copies:
        copy.start()

    def weights(slot, carry):
        here = pl.ds(pl.multiple_of(slot * slot_obs, 128), slot_obs)
        pltpu.make_async_copy(yh.at[here], yh.at[here], sem_y.at[slot, 0]).wait()
        pltpu.make_async_copy(yl.at[here], yl.at[here], sem_y.at[slot, 1]).wait()
        pltpu.make_async_copy(tap.at[here], tap.at[here], sem_y.at[slot, 2]).wait()
        cov = dot(yh[here, :], x_high[...]) + dot(yl[here, :], x_high[...])
        cov += dot(yh[here, :], x_low[...])
        kh[here, :], kl[here, :] = split(cov * tap[here, :])
        return carry

    lax.fori_loop(0, 3, weights, 0)
    pltpu.make_async_copy(w, w, sem_w).wait()
    blocks = band // ml

    def change(i, carry):
        at = pl.ds(pl.multiple_of(i * band, band), band)
        w_high, w_low = split(w[at, :])
        total[at, :] += dot(w_high, kh[...]) + dot(w_low, kh[...]) + dot(w_high, kl[...])
        for r in range(blocks):
            block = i * blocks + r
            pltpu.make_async_copy(
                total.at[pl.ds(pl.multiple_of(block * ml, ml), ml)],
                out.at[pl.ds(pl.multiple_of((me ^ block) * ml, ml), ml), pl.ds(start, width)],
                sem_out.at[block],
            ).start()
        return carry

    lax.fori_loop(0, members // band, change, 0)
    for block in range(local):
        pltpu.make_async_copy(
            total.at[pl.ds(block * ml, ml)],
            out.at[pl.ds(pl.multiple_of((me ^ block) * ml, ml), ml), pl.ds(start, width)],
            sem_out.at[block],
        ).wait()


def regroup_kernel(begin, side_ref, state_ref, keep_ref, give_ref, sem):
    blocks, ml, width = keep_ref.shape
    per_device = state_ref.shape[1] // (2 * blocks)
    side = side_ref[0]
    copies = []
    for ref, which in ((give_ref, 1 - side), (keep_ref, side)):
        for z in range(blocks):
            at = pl.multiple_of((2 * z + which) * per_device + begin, 128)
            copies.append(pltpu.make_async_copy(state_ref.at[:, pl.ds(at, width)], ref.at[z], sem))
    for copy in copies:
        copy.start()
    pltpu.make_async_copy(keep_ref, keep_ref, sem).wait()
    pltpu.make_async_copy(give_ref, give_ref, sem).wait()


def regroup(side, state, groups, begin, width):
    shape = jax.ShapeDtypeStruct((groups // 2, state.shape[0], width), f32)
    return pl.pallas_call(
        functools.partial(regroup_kernel, begin),
        out_shape=[shape] * 2,
        in_specs=[pl.BlockSpec(memory_space=pltpu.SMEM), anywhere],
        out_specs=[in_vmem] * 2,
        scratch_shapes=[pltpu.SemaphoreType.DMA],
        compiler_params=pltpu.CompilerParams(vmem_limit_bytes=vmem_limit),
        cost_estimate=small_cost,
    )(side, state)


def pair_kernel(begin, a_ref, b_ref, out_ref, sem):
    here = pl.ds(begin, out_ref.shape[3])
    copies = []
    for z in range(a_ref.shape[0]):
        copies.append(pltpu.make_async_copy(a_ref.at[z, :, here], out_ref.at[z, 0], sem))
        copies.append(pltpu.make_async_copy(b_ref.at[z, :, here], out_ref.at[z, 1], sem))
    for copy in copies:
        copy.start()
    pltpu.make_async_copy(out_ref, out_ref, sem).wait()


def pair(a, b, begin, width):
    return pl.pallas_call(
        functools.partial(pair_kernel, begin),
        out_shape=jax.ShapeDtypeStruct((a.shape[0], 2, a.shape[1], width), f32),
        in_specs=[anywhere] * 2,
        out_specs=in_vmem,
        scratch_shapes=[pltpu.SemaphoreType.DMA],
        compiler_params=pltpu.CompilerParams(vmem_limit_bytes=vmem_limit),
        cost_estimate=small_cost,
    )(a, b)


def update(me, points, obs, parts, innov, order, taper, out, start, per_device):
    members, width = 2 * points.shape[0] * points.shape[2], points.shape[3]
    window_obs = taper.shape[0]
    first = out is None
    operands = [me, points, *[o[0] for o in obs], *[o[1] for o in obs], *innov, taper]
    operands += [] if first else [out]
    return pl.pallas_call(
        functools.partial(update_kernel, parts, order, first, start),
        out_shape=jax.ShapeDtypeStruct((members, per_device), f32),
        in_specs=[pl.BlockSpec(memory_space=pltpu.SMEM)] + [anywhere] * (len(operands) - 1),
        out_specs=anywhere,
        scratch_shapes=[
            pltpu.VMEM((members, width), f32),
            pltpu.VMEM((members, width), bf16),
            pltpu.VMEM((members, width), bf16),
            pltpu.VMEM((window_obs, members), bf16),
            pltpu.VMEM((window_obs, members), bf16),
            pltpu.VMEM((members, window_obs), f32),
            pltpu.VMEM((window_obs, width), f32),
            pltpu.VMEM((window_obs, width), bf16),
            pltpu.VMEM((window_obs, width), bf16),
            pltpu.SemaphoreType.DMA,
            pltpu.SemaphoreType.DMA((3, 3)),
            pltpu.SemaphoreType.DMA,
            pltpu.SemaphoreType.DMA((len(order),)),
        ],
        input_output_aliases={} if first else {len(operands) - 1: 0},
        compiler_params=pltpu.CompilerParams(vmem_limit_bytes=vmem_limit),
        cost_estimate=small_cost,
    )(*operands)


def shards(state, obs_ensemble, innovations, obs_coords, tile_list, tile_counts):
    ml = state.shape[0]
    groups = lax.axis_size("mem")
    domains = lax.axis_size("dom")
    per_domain = state.shape[1]
    per_device = per_domain // groups
    obs_local = obs_ensemble.shape[1]
    members = ml * groups
    me = lax.axis_index("mem")
    domain = lax.axis_index("dom")
    odd = domain % 2

    bits = []
    b = groups // 2
    while b >= 1:
        bits.append(b)
        b //= 2
    order = [0]
    for b in bits:
        order = order + [r ^ b for r in order]

    across = [((i + 1) % domains, (i + 2) % domains) for i in range(0, domains, 2)]
    across = across + [(t, s) for s, t in across]
    chip = [(i, i ^ 1) for i in range(domains)]

    def tapered(coord_beside, coord_beyond):
        position = jnp.stack([jnp.int32(1), 2 - 2 * odd, 2 * odd]).astype(jnp.int32)
        coords = jnp.concatenate([obs_coords, coord_beside, coord_beyond], axis=1)
        nblocks = per_device // tile_side
        window = obs_local // tile_side
        point_ids, obs_ids = tile_list[0, 0, 0], tile_list[0, 0, 1]
        slots = point_ids.shape[0]
        live = (jnp.arange(slots, dtype=jnp.int32) < tile_counts[0, 0]).astype(f32)
        block_ids = (position[:, None] * window + jnp.arange(window, dtype=jnp.int32)[None]).reshape(-1)
        by_obs = (obs_ids[None, :] == block_ids[:, None]).astype(f32) * live[None]
        by_point = (point_ids[:, None] == jnp.arange(nblocks, dtype=jnp.int32)[None]).astype(f32)
        mask = jnp.sum(by_obs[:, :, None] * by_point[None], axis=1)
        mask = jnp.repeat(mask, tile_side, axis=1) / (members - 1)
        within = me * per_device + jnp.arange(per_device, dtype=jnp.int32)
        point_x = domain.astype(f32) + ((within % 32).astype(f32) + 0.5) / 32.0
        point_y = ((within // 32).astype(f32) + 0.5) / float(per_domain // 32)
        gap_x = jnp.abs(point_x[None, :] - coords[0][:, None])
        gap_x = jnp.minimum(gap_x, float(domains) - gap_x)
        gap_y = point_y[None, :] - coords[1][:, None]
        taper = jnp.exp(-(gap_x * gap_x + gap_y * gap_y) / (2.0 * taper_reach * taper_reach))
        taper = (taper.reshape(-1, tile_side, per_device) * mask[:, None, :]).reshape(-1, per_device)
        return taper

    edges = [per_device * e // 8 for e in span_edges]
    spans = [(edges[c], edges[c + 1] - edges[c]) for c in range(len(edges) - 1)]
    sides = [[i for i in range(groups) if i % 2 == s] for s in range(2)]
    my_side = (me % 2).astype(jnp.int32).reshape(1)

    keep, give = regroup(my_side, state, groups, 0, per_device)

    def assembled(halves, *deps):
        return lax.all_to_all(
            after(halves, *deps),
            "mem",
            split_axis=0,
            concat_axis=0,
            tiled=True,
            axis_index_groups=sides,
        )

    def far_gathered(x, *deps):
        x, got = x[None], []
        for b in bits[:-1]:
            got.append(swap(after(x, *deps), "mem", b))
            x = join(x, got[-1])
            deps = ()
        return x, got

    def cross(x, *deps):
        return lax.ppermute(after(x, *deps), "dom", across)

    def beside(x, *deps):
        return lax.ppermute(after(x, *deps), "dom", chip)

    def side(x, *deps):
        return swap(after(x, *deps), "mem", 1)

    got = side(give)
    obs_near, obs_got = far_gathered(obs_ensemble)
    inn_near, inn_got = far_gathered(innovations, obs_got[0])
    coord_beside = beside(obs_coords, obs_got[0])
    coord_beyond = cross(obs_coords, obs_got[0])
    taper = tapered(coord_beside, coord_beyond)
    obs_near_beyond = cross(obs_near, coord_beyond)
    obs_far = side(obs_near)
    paired = [pair(keep, got, *span) for span in spans]
    points = [assembled(paired[0], obs_got[-1], inn_got[-1])]
    obs_near_beside = beside(obs_near, obs_near_beyond, obs_far)
    inn_near_beyond = cross(inn_near, obs_near_beside, taper, paired[1])
    inn_far = side(inn_near, obs_near_beside)
    obs_far_beside = beside(obs_far, obs_near_beside)
    ready_own = prep_obs((obs_near, obs_far), order)
    ready_beside = prep_obs((obs_near_beside, obs_far_beside), order)
    obs_far_beyond = cross(obs_far, inn_near_beyond, inn_far, obs_far_beside, ready_own[0])
    inn_far_beyond = side(inn_near_beyond, inn_far)
    inn_near_beside = beside(inn_near, obs_far_beyond, inn_far_beyond, ready_beside[0])
    inn_far_beside = beside(inn_far, inn_near_beside)
    points.append(assembled(paired[1], points[0]))
    ready_beyond = prep_obs((obs_near_beyond, obs_far_beyond), order)
    obs = [ready_own, ready_beside, ready_beyond]
    innov = [inn_near, inn_far, inn_near_beside, inn_far_beside, inn_near_beyond, inn_far_beyond]
    parts = [(slot, slot * obs_local, obs_local) for slot in range(3)]
    out = None
    for c in range(len(spans)):
        out = update(
            me.astype(jnp.int32).reshape(1),
            points[c],
            obs,
            parts,
            innov,
            order,
            taper,
            out,
            spans[c][0],
            per_device,
        )
    return out


def solution(mesh):
    return jax.shard_map(
        shards,
        mesh=mesh,
        in_specs=(
            P("mem", "dom"),
            P("mem", "dom"),
            P("mem", "dom"),
            P(None, "dom"),
            P("dom", "mem", None, None),
            P("dom", "mem"),
        ),
        out_specs=P(None, ("dom", "mem")),
        check_vma=False,
    )
```

```python
import functools

import jax
import jax.numpy as jnp
from jax import lax
from jax.experimental import pallas as pl
from jax.experimental.pallas import tpu as pltpu
from jax.sharding import PartitionSpec as P

taper_reach = 0.6
tile_side = 128
f32, bf16 = jnp.float32, jnp.bfloat16
anywhere = pl.BlockSpec(memory_space=pl.ANY)
in_vmem = pl.BlockSpec(memory_space=pltpu.VMEM)
span_edges = (0, 6, 8)
small_cost = pl.CostEstimate(flops=1000, bytes_accessed=1000, transcendentals=0)
vmem_limit = 56 * 1024 * 1024


def dot(a, b):
    return lax.dot_general(a, b, (((1,), (0,)), ((), ())), preferred_element_type=f32)


def split(x):
    high = x.astype(bf16)
    return high, (x - high.astype(f32)).astype(bf16)


def swap(x, axis, distance):
    size = lax.axis_size(axis)
    return lax.ppermute(x, axis, [(i, i ^ distance) for i in range(size)])


def after(x, *deps):
    return lax.optimization_barrier((x, *deps))[0] if deps else x


def join_kernel(*refs):
    out_ref, sem = refs[-2:]
    at = 0
    for ref in refs[:-2]:
        size = ref.shape[0]
        pltpu.make_async_copy(ref, out_ref.at[pl.ds(at, size)], sem).start()
        at += size
    pltpu.make_async_copy(out_ref, out_ref, sem).wait()


def join(*blocks):
    count = sum(block.shape[0] for block in blocks)
    return pl.pallas_call(
        join_kernel,
        out_shape=jax.ShapeDtypeStruct((count, *blocks[0].shape[1:]), f32),
        in_specs=[anywhere] * len(blocks),
        out_specs=in_vmem,
        scratch_shapes=[pltpu.SemaphoreType.DMA],
        compiler_params=pltpu.CompilerParams(vmem_limit_bytes=vmem_limit),
        cost_estimate=small_cost,
    )(*blocks)


def prep_obs_kernel(order, near_ref, far_ref, high_ref, low_ref):
    blocks, rows, width = near_ref.shape
    refs = [near_ref.at[i] for i in range(blocks)] + [far_ref.at[i] for i in range(blocks)]
    total = jnp.zeros((1, width), f32)
    for ref in refs:
        total += jnp.sum(ref[...], axis=0, keepdims=True)
    mean = total / (2 * blocks * rows)
    for i, ref in enumerate(refs):
        high, low = split((ref[...] - mean).T)
        at = pl.ds(order[i] * rows, rows)
        high_ref[:, at] = high
        low_ref[:, at] = low


def prep_obs(pair, order):
    blocks, rows, width = pair[0].shape
    band = 256 if width % 256 == 0 else 128
    whole = pl.BlockSpec((blocks, rows, band), lambda j: (0, 0, j))
    return pl.pallas_call(
        functools.partial(prep_obs_kernel, order),
        grid=(width // band,),
        out_shape=[jax.ShapeDtypeStruct((width, 2 * blocks * rows), bf16)] * 2,
        in_specs=[whole] * 2,
        out_specs=[pl.BlockSpec((band, 2 * blocks * rows), lambda j: (j, 0))] * 2,
        compiler_params=pltpu.CompilerParams(vmem_limit_bytes=vmem_limit),
        cost_estimate=small_cost,
    )(*pair)


def update_kernel(parts, order, first, start, *refs):
    me_ref, points, refs = refs[0], refs[1], refs[2:]
    me = me_ref[0]
    nobs = len(parts)
    obs_high, refs = refs[:nobs], refs[nobs:]
    obs_low, refs = refs[:nobs], refs[nobs:]
    ninn = len(refs) - (15 if first else 16)
    inn, refs = refs[:ninn], refs[ninn:]
    taper = refs[0]
    refs = refs[1 if first else 2 :]
    out, total, x_high, x_low, yh, yl, w, tap, kh, kl, sem_x, sem_y, sem_w, sem_out = refs
    members, width = total.shape
    local = len(order)
    ml = members // local
    window = tap.shape[0]
    slot_obs = window // 3
    band = min(512, members)
    x_copies = []
    for r in range(local):
        paired = len(points.shape) == 4
        block = points.at[lax.div(me ^ r, 2), r % 2] if paired else points.at[me ^ r]
        x_copies.append(pltpu.make_async_copy(block, total.at[pl.ds(r * ml, ml)], sem_x))
    y_copies = []
    for i, (slot, at, size) in enumerate(parts):
        here = pl.ds(at, size)
        y_copies.append(
            [
                pltpu.make_async_copy(obs_high[i], yh.at[here], sem_y.at[slot, 0]),
                pltpu.make_async_copy(obs_low[i], yl.at[here], sem_y.at[slot, 1]),
                pltpu.make_async_copy(
                    taper.at[here, pl.ds(start, width)], tap.at[here], sem_y.at[slot, 2]
                ),
            ]
        )
    w_copies = []
    for i in range(ninn):
        slot, part = i // 2, i % 2
        here = pl.ds(slot * slot_obs, slot_obs)
        for k in range(local // 2):
            at = pl.ds(order[part * (local // 2) + k] * ml, ml)
            w_copies.append(pltpu.make_async_copy(inn[i].at[k], w.at[at, here], sem_w))
    for copy in x_copies + y_copies[0]:
        copy.start()
    pltpu.make_async_copy(total, total, sem_x).wait()

    def halves(i, carry):
        at = pl.ds(pl.multiple_of(i * 128, 128), 128)
        x_high[at, :], x_low[at, :] = split(total[at, :])
        return carry

    lax.fori_loop(0, members // 128, halves, 0)
    for copy in y_copies[1] + y_copies[2] + w_copies:
        copy.start()

    def weights(slot, carry):
        here = pl.ds(pl.multiple_of(slot * slot_obs, 128), slot_obs)
        pltpu.make_async_copy(yh.at[here], yh.at[here], sem_y.at[slot, 0]).wait()
        pltpu.make_async_copy(yl.at[here], yl.at[here], sem_y.at[slot, 1]).wait()
        pltpu.make_async_copy(tap.at[here], tap.at[here], sem_y.at[slot, 2]).wait()
        cov = dot(yh[here, :], x_high[...]) + dot(yl[here, :], x_high[...])
        cov += dot(yh[here, :], x_low[...])
        kh[here, :], kl[here, :] = split(cov * tap[here, :])
        return carry

    lax.fori_loop(0, 3, weights, 0)
    pltpu.make_async_copy(w, w, sem_w).wait()
    blocks = band // ml

    def change(i, carry):
        at = pl.ds(pl.multiple_of(i * band, band), band)
        w_high, w_low = split(w[at, :])
        total[at, :] += dot(w_high, kh[...]) + dot(w_low, kh[...]) + dot(w_high, kl[...])
        for r in range(blocks):
            block = i * blocks + r
            pltpu.make_async_copy(
                total.at[pl.ds(pl.multiple_of(block * ml, ml), ml)],
                out.at[pl.ds(pl.multiple_of((me ^ block) * ml, ml), ml), pl.ds(start, width)],
                sem_out.at[block],
            ).start()
        return carry

    lax.fori_loop(0, members // band, change, 0)
    for block in range(local):
        pltpu.make_async_copy(
            total.at[pl.ds(block * ml, ml)],
            out.at[pl.ds(pl.multiple_of((me ^ block) * ml, ml), ml), pl.ds(start, width)],
            sem_out.at[block],
        ).wait()


def side_copies(side, state_ref, begin, out_refs, sem):
    width = out_refs[0].shape[1]
    per_device = state_ref.shape[1] // (2 * len(out_refs))
    copies = []
    for z, out_ref in enumerate(out_refs):
        at = pl.multiple_of((2 * z + side) * per_device + begin, 128)
        copies.append(pltpu.make_async_copy(state_ref.at[:, pl.ds(at, width)], out_ref, sem))
    return copies


def given_kernel(begin, side_ref, state_ref, out_ref, sem):
    refs = [out_ref.at[z] for z in range(out_ref.shape[0])]
    for copy in side_copies(1 - side_ref[0], state_ref, begin, refs, sem):
        copy.start()
    pltpu.make_async_copy(out_ref, out_ref, sem).wait()


def given(side, state, groups, begin, width):
    return pl.pallas_call(
        functools.partial(given_kernel, begin),
        out_shape=jax.ShapeDtypeStruct((groups // 2, state.shape[0], width), f32),
        in_specs=[pl.BlockSpec(memory_space=pltpu.SMEM), anywhere],
        out_specs=in_vmem,
        scratch_shapes=[pltpu.SemaphoreType.DMA],
        compiler_params=pltpu.CompilerParams(vmem_limit_bytes=vmem_limit),
        cost_estimate=small_cost,
    )(side, state)


def regroup_kernel(begin, state_ref, out_ref, sem):
    groups, ml, width = out_ref.shape
    per_device = state_ref.shape[1] // groups
    for g in range(groups):
        here = pl.ds(g * per_device + begin, width)
        pltpu.make_async_copy(state_ref.at[:, here], out_ref.at[g], sem).start()
    pltpu.make_async_copy(out_ref, out_ref, sem).wait()


def regroup(state, groups, begin, width):
    return pl.pallas_call(
        functools.partial(regroup_kernel, begin),
        out_shape=jax.ShapeDtypeStruct((groups, state.shape[0], width), f32),
        in_specs=[anywhere],
        out_specs=in_vmem,
        scratch_shapes=[pltpu.SemaphoreType.DMA],
        compiler_params=pltpu.CompilerParams(vmem_limit_bytes=vmem_limit),
        cost_estimate=small_cost,
    )(state)


def pair_kernel(begin, side_ref, state_ref, got_ref, out_ref, sem):
    blocks = out_ref.shape[0]
    copies = side_copies(
        side_ref[0], state_ref, begin, [out_ref.at[z, 0] for z in range(blocks)], sem
    )
    for z in range(blocks):
        copies.append(pltpu.make_async_copy(got_ref.at[z], out_ref.at[z, 1], sem))
    for copy in copies:
        copy.start()
    pltpu.make_async_copy(out_ref, out_ref, sem).wait()


def pair(side, state, got, begin):
    blocks, ml, width = got.shape
    return pl.pallas_call(
        functools.partial(pair_kernel, begin),
        out_shape=jax.ShapeDtypeStruct((blocks, 2, ml, width), f32),
        in_specs=[pl.BlockSpec(memory_space=pltpu.SMEM), anywhere, anywhere],
        out_specs=in_vmem,
        scratch_shapes=[pltpu.SemaphoreType.DMA],
        compiler_params=pltpu.CompilerParams(vmem_limit_bytes=vmem_limit),
        cost_estimate=small_cost,
    )(side, state, got)


def update(me, points, obs, parts, innov, order, taper, out, start, per_device):
    width = points.shape[-1]
    members = points.size // width
    window_obs = taper.shape[0]
    first = out is None
    operands = [me, points, *[o[0] for o in obs], *[o[1] for o in obs], *innov, taper]
    operands += [] if first else [out]
    return pl.pallas_call(
        functools.partial(update_kernel, parts, order, first, start),
        out_shape=jax.ShapeDtypeStruct((members, per_device), f32),
        in_specs=[pl.BlockSpec(memory_space=pltpu.SMEM)] + [anywhere] * (len(operands) - 1),
        out_specs=anywhere,
        scratch_shapes=[
            pltpu.VMEM((members, width), f32),
            pltpu.VMEM((members, width), bf16),
            pltpu.VMEM((members, width), bf16),
            pltpu.VMEM((window_obs, members), bf16),
            pltpu.VMEM((window_obs, members), bf16),
            pltpu.VMEM((members, window_obs), f32),
            pltpu.VMEM((window_obs, width), f32),
            pltpu.VMEM((window_obs, width), bf16),
            pltpu.VMEM((window_obs, width), bf16),
            pltpu.SemaphoreType.DMA,
            pltpu.SemaphoreType.DMA((3, 3)),
            pltpu.SemaphoreType.DMA,
            pltpu.SemaphoreType.DMA((len(order),)),
        ],
        input_output_aliases={} if first else {len(operands) - 1: 0},
        compiler_params=pltpu.CompilerParams(vmem_limit_bytes=vmem_limit),
        cost_estimate=small_cost,
    )(*operands)


def shards(state, obs_ensemble, innovations, obs_coords, tile_list, tile_counts):
    ml = state.shape[0]
    groups = lax.axis_size("mem")
    domains = lax.axis_size("dom")
    per_domain = state.shape[1]
    per_device = per_domain // groups
    obs_local = obs_ensemble.shape[1]
    members = ml * groups
    me = lax.axis_index("mem")
    domain = lax.axis_index("dom")
    odd = domain % 2

    bits = []
    b = groups // 2
    while b >= 1:
        bits.append(b)
        b //= 2
    order = [0]
    for b in bits:
        order = order + [r ^ b for r in order]

    across = [((i + 1) % domains, (i + 2) % domains) for i in range(0, domains, 2)]
    across = across + [(t, s) for s, t in across]
    chip = [(i, i ^ 1) for i in range(domains)]

    def tapered(coord_beside, coord_beyond):
        position = jnp.stack([jnp.int32(1), 2 - 2 * odd, 2 * odd]).astype(jnp.int32)
        coords = jnp.concatenate([obs_coords, coord_beside, coord_beyond], axis=1)
        nblocks = per_device // tile_side
        window = obs_local // tile_side
        point_ids, obs_ids = tile_list[0, 0, 0], tile_list[0, 0, 1]
        slots = point_ids.shape[0]
        live = (jnp.arange(slots, dtype=jnp.int32) < tile_counts[0, 0]).astype(f32)
        block_ids = (position[:, None] * window + jnp.arange(window, dtype=jnp.int32)[None]).reshape(-1)
        by_obs = (obs_ids[None, :] == block_ids[:, None]).astype(f32) * live[None]
        by_point = (point_ids[:, None] == jnp.arange(nblocks, dtype=jnp.int32)[None]).astype(f32)
        mask = jnp.sum(by_obs[:, :, None] * by_point[None], axis=1)
        mask = jnp.repeat(mask, tile_side, axis=1) / (members - 1)
        within = me * per_device + jnp.arange(per_device, dtype=jnp.int32)
        point_x = domain.astype(f32) + ((within % 32).astype(f32) + 0.5) / 32.0
        point_y = ((within // 32).astype(f32) + 0.5) / float(per_domain // 32)
        gap_x = jnp.abs(point_x[None, :] - coords[0][:, None])
        gap_x = jnp.minimum(gap_x, float(domains) - gap_x)
        gap_y = point_y[None, :] - coords[1][:, None]
        taper = jnp.exp(-(gap_x * gap_x + gap_y * gap_y) / (2.0 * taper_reach * taper_reach))
        taper = (taper.reshape(-1, tile_side, per_device) * mask[:, None, :]).reshape(-1, per_device)
        return taper

    edges = [per_device * e // 8 for e in span_edges]
    spans = [(edges[c], edges[c + 1] - edges[c]) for c in range(len(edges) - 1)]
    sides = [[i for i in range(groups) if i % 2 == s] for s in range(2)]
    my_side = (me % 2).astype(jnp.int32).reshape(1)

    def exchanged(span, *deps):
        return side(given(my_side, after(state, *deps), groups, *span))

    def assembled(blocks, within, *deps):
        return lax.all_to_all(
            after(blocks, *deps),
            "mem",
            split_axis=0,
            concat_axis=0,
            tiled=True,
            axis_index_groups=within,
        )

    def far_gathered(x, *deps):
        own, others, got = after(x[None], *deps), [], []
        early = swap(own, "mem", bits[-2])
        for b in bits[:-2]:
            got.append(swap(join(own, *others) if others else own, "mem", b))
            others.append(got[-1])
        got.append(swap(join(*others) if len(others) > 1 else others[0], "mem", bits[-2]))
        return join(own, *others, early, got[-1]), got

    def cross(x, *deps):
        return lax.ppermute(after(x, *deps), "dom", across)

    def beside(x, *deps):
        return lax.ppermute(after(x, *deps), "dom", chip)

    def side(x, *deps):
        return swap(after(x, *deps), "mem", 1)

    obs_near, obs_got = far_gathered(obs_ensemble)
    first = exchanged(spans[0])
    inn_near, inn_got = far_gathered(innovations, obs_got[0])
    coord_beside = beside(obs_coords, obs_got[0])
    coord_beyond = cross(obs_coords, obs_got[0])
    taper = tapered(coord_beside, coord_beyond)
    obs_near_beyond = cross(obs_near, coord_beyond, coord_beside)
    obs_far = side(obs_near)
    paired = pair(my_side, state, first, spans[0][0])
    points = [assembled(paired, sides, obs_got[-1], inn_got[-1])]
    obs_near_beside = beside(obs_near, obs_near_beyond, obs_far, taper, inn_near)
    pause = beside(obs_far, obs_near_beside)
    inn_near_beyond = cross(inn_near, pause)
    inn_far = side(inn_near, pause)
    obs_far_beside = pause
    ready_own = prep_obs((obs_near, obs_far), order)
    ready_beside = prep_obs((obs_near_beside, obs_far_beside), order)
    blocks = regroup(after(state, obs_got[-1]), groups, *spans[1])
    obs_far_beyond = cross(obs_far, inn_near_beyond, inn_far, obs_far_beside, ready_own[0], blocks)
    inn_far_beyond = side(inn_near_beyond, inn_far)
    inn_near_beside = beside(inn_near, obs_far_beyond, inn_far_beyond, ready_beside[0])
    inn_far_beside = beside(inn_far, inn_near_beside)
    points.append(assembled(blocks, None, points[0]))
    ready_beyond = prep_obs((obs_near_beyond, obs_far_beyond), order)
    obs = [ready_own, ready_beside, ready_beyond]
    innov = [inn_near, inn_far, inn_near_beside, inn_far_beside, inn_near_beyond, inn_far_beyond]
    parts = [(slot, slot * obs_local, obs_local) for slot in range(3)]
    out = None
    for c in range(len(spans)):
        out = update(
            me.astype(jnp.int32).reshape(1),
            points[c],
            obs,
            parts,
            innov,
            order,
            taper,
            out,
            spans[c][0],
            per_device,
        )
    return out


def solution(mesh):
    return jax.shard_map(
        shards,
        mesh=mesh,
        in_specs=(
            P("mem", "dom"),
            P("mem", "dom"),
            P("mem", "dom"),
            P(None, "dom"),
            P("dom", "mem", None, None),
            P("dom", "mem"),
        ),
        out_specs=P(None, ("dom", "mem")),
        check_vma=False,
    )
```

```python
import functools

import jax
import jax.numpy as jnp
from jax import lax
from jax.experimental import pallas as pl
from jax.experimental.pallas import tpu as pltpu
from jax.sharding import PartitionSpec as P

taper_reach = 0.6
tile_side = 128
f32, bf16 = jnp.float32, jnp.bfloat16
anywhere = pl.BlockSpec(memory_space=pl.ANY)
in_vmem = pl.BlockSpec(memory_space=pltpu.VMEM)
span_edges = (0, 6, 8)
small_cost = pl.CostEstimate(flops=1000, bytes_accessed=1000, transcendentals=0)
vmem_limit = 56 * 1024 * 1024


def dot(a, b):
    return lax.dot_general(a, b, (((1,), (0,)), ((), ())), preferred_element_type=f32)


def split(x):
    high = x.astype(bf16)
    return high, (x - high.astype(f32)).astype(bf16)


def swap(x, axis, distance):
    size = lax.axis_size(axis)
    return lax.ppermute(x, axis, [(i, i ^ distance) for i in range(size)])


def after(x, *deps):
    return lax.optimization_barrier((x, *deps))[0] if deps else x


def join_kernel(*refs):
    out_ref, sem = refs[-2:]
    at = 0
    for ref in refs[:-2]:
        size = ref.shape[0]
        pltpu.make_async_copy(ref, out_ref.at[pl.ds(at, size)], sem).start()
        at += size
    pltpu.make_async_copy(out_ref, out_ref, sem).wait()


def join(*blocks):
    count = sum(block.shape[0] for block in blocks)
    return pl.pallas_call(
        join_kernel,
        out_shape=jax.ShapeDtypeStruct((count, *blocks[0].shape[1:]), f32),
        in_specs=[anywhere] * len(blocks),
        out_specs=in_vmem,
        scratch_shapes=[pltpu.SemaphoreType.DMA],
        compiler_params=pltpu.CompilerParams(vmem_limit_bytes=vmem_limit),
        cost_estimate=small_cost,
    )(*blocks)


def prep_obs_kernel(order, near_ref, far_ref, high_ref, low_ref):
    blocks, rows, width = near_ref.shape
    refs = [near_ref.at[i] for i in range(blocks)] + [far_ref.at[i] for i in range(blocks)]
    total = jnp.zeros((1, width), f32)
    for ref in refs:
        total += jnp.sum(ref[...], axis=0, keepdims=True)
    mean = total / (2 * blocks * rows)
    for i, ref in enumerate(refs):
        high, low = split((ref[...] - mean).T)
        at = pl.ds(order[i] * rows, rows)
        high_ref[:, at] = high
        low_ref[:, at] = low


def prep_obs(pair, order):
    blocks, rows, width = pair[0].shape
    band = 256 if width % 256 == 0 else 128
    whole = pl.BlockSpec((blocks, rows, band), lambda j: (0, 0, j))
    return pl.pallas_call(
        functools.partial(prep_obs_kernel, order),
        grid=(width // band,),
        out_shape=[jax.ShapeDtypeStruct((width, 2 * blocks * rows), bf16)] * 2,
        in_specs=[whole] * 2,
        out_specs=[pl.BlockSpec((band, 2 * blocks * rows), lambda j: (j, 0))] * 2,
        compiler_params=pltpu.CompilerParams(vmem_limit_bytes=vmem_limit),
        cost_estimate=small_cost,
    )(*pair)


def update_kernel(parts, order, first, start, *refs):
    me_ref, points, refs = refs[0], refs[1], refs[2:]
    me = me_ref[0]
    nobs = len(parts)
    obs_high, refs = refs[:nobs], refs[nobs:]
    obs_low, refs = refs[:nobs], refs[nobs:]
    ninn = len(refs) - (15 if first else 16)
    inn, refs = refs[:ninn], refs[ninn:]
    taper = refs[0]
    refs = refs[1 if first else 2 :]
    out, total, x_high, x_low, yh, yl, w, tap, kh, kl, sem_x, sem_y, sem_w, sem_out = refs
    members, width = total.shape
    local = len(order)
    ml = members // local
    window = tap.shape[0]
    slot_obs = window // 3
    band = min(512, members)
    x_copies = []
    for r in range(local):
        paired = len(points.shape) == 4
        block = points.at[lax.div(me ^ r, 2), r % 2] if paired else points.at[me ^ r]
        x_copies.append(pltpu.make_async_copy(block, total.at[pl.ds(r * ml, ml)], sem_x))
    y_copies = []
    for i, (slot, at, size) in enumerate(parts):
        here = pl.ds(at, size)
        y_copies.append(
            [
                pltpu.make_async_copy(obs_high[i], yh.at[here], sem_y.at[slot, 0]),
                pltpu.make_async_copy(obs_low[i], yl.at[here], sem_y.at[slot, 1]),
                pltpu.make_async_copy(
                    taper.at[here, pl.ds(start, width)], tap.at[here], sem_y.at[slot, 2]
                ),
            ]
        )
    w_copies = []
    for i in range(ninn):
        slot, part = i // 2, i % 2
        here = pl.ds(slot * slot_obs, slot_obs)
        for k in range(local // 2):
            at = pl.ds(order[part * (local // 2) + k] * ml, ml)
            w_copies.append(pltpu.make_async_copy(inn[i].at[k], w.at[at, here], sem_w))
    for copy in x_copies + y_copies[0]:
        copy.start()
    pltpu.make_async_copy(total, total, sem_x).wait()

    def halves(i, carry):
        at = pl.ds(pl.multiple_of(i * 128, 128), 128)
        x_high[at, :], x_low[at, :] = split(total[at, :])
        return carry

    lax.fori_loop(0, members // 128, halves, 0)
    for copy in y_copies[1] + y_copies[2] + w_copies:
        copy.start()

    def weights(slot, carry):
        here = pl.ds(pl.multiple_of(slot * slot_obs, 128), slot_obs)
        pltpu.make_async_copy(yh.at[here], yh.at[here], sem_y.at[slot, 0]).wait()
        pltpu.make_async_copy(yl.at[here], yl.at[here], sem_y.at[slot, 1]).wait()
        pltpu.make_async_copy(tap.at[here], tap.at[here], sem_y.at[slot, 2]).wait()
        cov = dot(yh[here, :], x_high[...]) + dot(yl[here, :], x_high[...])
        cov += dot(yh[here, :], x_low[...])
        kh[here, :], kl[here, :] = split(cov * tap[here, :])
        return carry

    lax.fori_loop(0, 3, weights, 0)
    pltpu.make_async_copy(w, w, sem_w).wait()
    blocks = band // ml

    def change(i, carry):
        at = pl.ds(pl.multiple_of(i * band, band), band)
        w_high, w_low = split(w[at, :])
        total[at, :] += dot(w_high, kh[...]) + dot(w_low, kh[...]) + dot(w_high, kl[...])
        for r in range(blocks):
            block = i * blocks + r
            pltpu.make_async_copy(
                total.at[pl.ds(pl.multiple_of(block * ml, ml), ml)],
                out.at[pl.ds(pl.multiple_of((me ^ block) * ml, ml), ml), pl.ds(start, width)],
                sem_out.at[block],
            ).start()
        return carry

    lax.fori_loop(0, members // band, change, 0)
    for block in range(local):
        pltpu.make_async_copy(
            total.at[pl.ds(block * ml, ml)],
            out.at[pl.ds(pl.multiple_of((me ^ block) * ml, ml), ml), pl.ds(start, width)],
            sem_out.at[block],
        ).wait()


def side_copies(side, state_ref, begin, out_refs, sem):
    width = out_refs[0].shape[1]
    per_device = state_ref.shape[1] // (2 * len(out_refs))
    copies = []
    for z, out_ref in enumerate(out_refs):
        at = pl.multiple_of((2 * z + side) * per_device + begin, 128)
        copies.append(pltpu.make_async_copy(state_ref.at[:, pl.ds(at, width)], out_ref, sem))
    return copies


def given_kernel(begin, side_ref, state_ref, out_ref, sem):
    refs = [out_ref.at[z] for z in range(out_ref.shape[0])]
    for copy in side_copies(1 - side_ref[0], state_ref, begin, refs, sem):
        copy.start()
    pltpu.make_async_copy(out_ref, out_ref, sem).wait()


def given(side, state, groups, begin, width):
    return pl.pallas_call(
        functools.partial(given_kernel, begin),
        out_shape=jax.ShapeDtypeStruct((groups // 2, state.shape[0], width), f32),
        in_specs=[pl.BlockSpec(memory_space=pltpu.SMEM), anywhere],
        out_specs=in_vmem,
        scratch_shapes=[pltpu.SemaphoreType.DMA],
        compiler_params=pltpu.CompilerParams(vmem_limit_bytes=vmem_limit),
        cost_estimate=small_cost,
    )(side, state)


def regroup_kernel(begin, state_ref, out_ref, sem):
    groups, ml, width = out_ref.shape
    per_device = state_ref.shape[1] // groups
    for g in range(groups):
        here = pl.ds(g * per_device + begin, width)
        pltpu.make_async_copy(state_ref.at[:, here], out_ref.at[g], sem).start()
    pltpu.make_async_copy(out_ref, out_ref, sem).wait()


def regroup(state, groups, begin, width):
    return pl.pallas_call(
        functools.partial(regroup_kernel, begin),
        out_shape=jax.ShapeDtypeStruct((groups, state.shape[0], width), f32),
        in_specs=[anywhere],
        out_specs=in_vmem,
        scratch_shapes=[pltpu.SemaphoreType.DMA],
        compiler_params=pltpu.CompilerParams(vmem_limit_bytes=vmem_limit),
        cost_estimate=small_cost,
    )(state)


def kept_kernel(begin, side_ref, state_ref, out_ref, held, sem_in, sem_out):
    blocks = held.shape[0]
    refs = [held.at[z] for z in range(blocks)]
    for copy in side_copies(side_ref[0], state_ref, begin, refs, sem_in):
        copy.start()
    pltpu.make_async_copy(held, held, sem_in).wait()
    for z in range(blocks):
        pltpu.make_async_copy(held.at[z], out_ref.at[z, 0], sem_out).start()
    pltpu.make_async_copy(held, held, sem_out).wait()


def kept(side, state, groups, begin, width):
    blocks, ml = groups // 2, state.shape[0]
    return pl.pallas_call(
        functools.partial(kept_kernel, begin),
        out_shape=jax.ShapeDtypeStruct((blocks, 2, ml, width), f32),
        in_specs=[pl.BlockSpec(memory_space=pltpu.SMEM), anywhere],
        out_specs=anywhere,
        scratch_shapes=[
            pltpu.VMEM((blocks, ml, width), f32),
            pltpu.SemaphoreType.DMA,
            pltpu.SemaphoreType.DMA,
        ],
        compiler_params=pltpu.CompilerParams(vmem_limit_bytes=vmem_limit),
        cost_estimate=small_cost,
    )(side, state)


def filled_kernel(got_ref, old_ref, out_ref, held, sem_in, sem_out):
    pltpu.make_async_copy(got_ref, held, sem_in).start()
    pltpu.make_async_copy(held, held, sem_in).wait()
    for z in range(held.shape[0]):
        pltpu.make_async_copy(held.at[z], out_ref.at[z, 1], sem_out).start()
    pltpu.make_async_copy(held, held, sem_out).wait()


def filled(got, old):
    return pl.pallas_call(
        filled_kernel,
        out_shape=jax.ShapeDtypeStruct(old.shape, f32),
        in_specs=[anywhere, anywhere],
        out_specs=anywhere,
        scratch_shapes=[
            pltpu.VMEM(got.shape, f32),
            pltpu.SemaphoreType.DMA,
            pltpu.SemaphoreType.DMA,
        ],
        input_output_aliases={1: 0},
        compiler_params=pltpu.CompilerParams(vmem_limit_bytes=vmem_limit),
        cost_estimate=small_cost,
    )(got, old)


def update(me, points, obs, parts, innov, order, taper, out, start, per_device):
    width = points.shape[-1]
    members = points.size // width
    window_obs = taper.shape[0]
    first = out is None
    operands = [me, points, *[o[0] for o in obs], *[o[1] for o in obs], *innov, taper]
    operands += [] if first else [out]
    return pl.pallas_call(
        functools.partial(update_kernel, parts, order, first, start),
        out_shape=jax.ShapeDtypeStruct((members, per_device), f32),
        in_specs=[pl.BlockSpec(memory_space=pltpu.SMEM)] + [anywhere] * (len(operands) - 1),
        out_specs=anywhere,
        scratch_shapes=[
            pltpu.VMEM((members, width), f32),
            pltpu.VMEM((members, width), bf16),
            pltpu.VMEM((members, width), bf16),
            pltpu.VMEM((window_obs, members), bf16),
            pltpu.VMEM((window_obs, members), bf16),
            pltpu.VMEM((members, window_obs), f32),
            pltpu.VMEM((window_obs, width), f32),
            pltpu.VMEM((window_obs, width), bf16),
            pltpu.VMEM((window_obs, width), bf16),
            pltpu.SemaphoreType.DMA,
            pltpu.SemaphoreType.DMA((3, 3)),
            pltpu.SemaphoreType.DMA,
            pltpu.SemaphoreType.DMA((len(order),)),
        ],
        input_output_aliases={} if first else {len(operands) - 1: 0},
        compiler_params=pltpu.CompilerParams(vmem_limit_bytes=vmem_limit),
        cost_estimate=small_cost,
    )(*operands)


def shards(state, obs_ensemble, innovations, obs_coords, tile_list, tile_counts):
    ml = state.shape[0]
    groups = lax.axis_size("mem")
    domains = lax.axis_size("dom")
    per_domain = state.shape[1]
    per_device = per_domain // groups
    obs_local = obs_ensemble.shape[1]
    members = ml * groups
    me = lax.axis_index("mem")
    domain = lax.axis_index("dom")
    odd = domain % 2

    bits = []
    b = groups // 2
    while b >= 1:
        bits.append(b)
        b //= 2
    order = [0]
    for b in bits:
        order = order + [r ^ b for r in order]

    across = [((i + 1) % domains, (i + 2) % domains) for i in range(0, domains, 2)]
    across = across + [(t, s) for s, t in across]
    chip = [(i, i ^ 1) for i in range(domains)]

    def tapered(coord_beside, coord_beyond):
        position = jnp.stack([jnp.int32(1), 2 - 2 * odd, 2 * odd]).astype(jnp.int32)
        coords = jnp.concatenate([obs_coords, coord_beside, coord_beyond], axis=1)
        nblocks = per_device // tile_side
        window = obs_local // tile_side
        point_ids, obs_ids = tile_list[0, 0, 0], tile_list[0, 0, 1]
        slots = point_ids.shape[0]
        live = (jnp.arange(slots, dtype=jnp.int32) < tile_counts[0, 0]).astype(f32)
        block_ids = (position[:, None] * window + jnp.arange(window, dtype=jnp.int32)[None]).reshape(-1)
        by_obs = (obs_ids[None, :] == block_ids[:, None]).astype(f32) * live[None]
        by_point = (point_ids[:, None] == jnp.arange(nblocks, dtype=jnp.int32)[None]).astype(f32)
        mask = jnp.sum(by_obs[:, :, None] * by_point[None], axis=1)
        mask = jnp.repeat(mask, tile_side, axis=1) / (members - 1)
        within = me * per_device + jnp.arange(per_device, dtype=jnp.int32)
        point_x = domain.astype(f32) + ((within % 32).astype(f32) + 0.5) / 32.0
        point_y = ((within // 32).astype(f32) + 0.5) / float(per_domain // 32)
        gap_x = jnp.abs(point_x[None, :] - coords[0][:, None])
        gap_x = jnp.minimum(gap_x, float(domains) - gap_x)
        gap_y = point_y[None, :] - coords[1][:, None]
        taper = jnp.exp(-(gap_x * gap_x + gap_y * gap_y) / (2.0 * taper_reach * taper_reach))
        taper = (taper.reshape(-1, tile_side, per_device) * mask[:, None, :]).reshape(-1, per_device)
        return taper

    edges = [per_device * e // 8 for e in span_edges]
    spans = [(edges[c], edges[c + 1] - edges[c]) for c in range(len(edges) - 1)]
    sides = [[i for i in range(groups) if i % 2 == s] for s in range(2)]
    my_side = (me % 2).astype(jnp.int32).reshape(1)

    def assembled(blocks, within, *deps):
        return lax.all_to_all(
            after(blocks, *deps),
            "mem",
            split_axis=0,
            concat_axis=0,
            tiled=True,
            axis_index_groups=within,
        )

    def far_gathered(x, ahead, *deps):
        own, others, got = after(x[None], *deps), [], []
        early = swap(own if ahead is None else after(own, ahead), "mem", bits[-2])
        for b in bits[:-2]:
            got.append(swap(join(own, *others) if others else own, "mem", b))
            others.append(got[-1])
        got.append(swap(join(*others) if len(others) > 1 else others[0], "mem", bits[-2]))
        return join(own, *others, early, got[-1]), got

    def cross(x, *deps):
        return lax.ppermute(after(x, *deps), "dom", across)

    def beside(x, *deps):
        return lax.ppermute(after(x, *deps), "dom", chip)

    def side(x, *deps):
        return swap(after(x, *deps), "mem", 1)

    give = given(my_side, state, groups, *spans[0])
    first = side(give)
    obs_near, obs_got = far_gathered(obs_ensemble, give)
    inn_near, inn_got = far_gathered(innovations, None, obs_got[0])
    coord_beside = beside(obs_coords, obs_got[0])
    coord_beyond = cross(obs_coords, obs_got[0])
    taper = tapered(coord_beside, coord_beyond)
    obs_near_beyond = cross(obs_near, coord_beyond, coord_beside)
    obs_far = side(obs_near)
    paired = filled(first, kept(my_side, state, groups, *spans[0]))
    points = [assembled(paired, sides, obs_got[-1], inn_got[-1])]
    obs_near_beside = beside(obs_near, obs_near_beyond, obs_far, taper, inn_near)
    pause = beside(obs_far, obs_near_beside)
    inn_near_beyond = cross(inn_near, pause)
    inn_far = side(inn_near, pause)
    obs_far_beside = pause
    ready_own = prep_obs((obs_near, obs_far), order)
    ready_beside = prep_obs((obs_near_beside, obs_far_beside), order)
    blocks = regroup(after(state, obs_got[-1]), groups, *spans[1])
    obs_far_beyond = cross(obs_far, inn_near_beyond, inn_far, obs_far_beside, ready_own[0], blocks)
    inn_far_beyond = side(inn_near_beyond, inn_far)
    inn_near_beside = beside(inn_near, obs_far_beyond, inn_far_beyond, ready_beside[0])
    inn_far_beside = beside(inn_far, inn_near_beside)
    points.append(assembled(blocks, None, points[0]))
    ready_beyond = prep_obs((obs_near_beyond, obs_far_beyond), order)
    obs = [ready_own, ready_beside, ready_beyond]
    innov = [inn_near, inn_far, inn_near_beside, inn_far_beside, inn_near_beyond, inn_far_beyond]
    parts = [(slot, slot * obs_local, obs_local) for slot in range(3)]
    out = None
    for c in range(len(spans)):
        out = update(
            me.astype(jnp.int32).reshape(1),
            points[c],
            obs,
            parts,
            innov,
            order,
            taper,
            out,
            spans[c][0],
            per_device,
        )
    return out


def solution(mesh):
    return jax.shard_map(
        shards,
        mesh=mesh,
        in_specs=(
            P("mem", "dom"),
            P("mem", "dom"),
            P("mem", "dom"),
            P(None, "dom"),
            P("dom", "mem", None, None),
            P("dom", "mem"),
        ),
        out_specs=P(None, ("dom", "mem")),
        check_vma=False,
    )
```

```python
import functools

import jax
import jax.numpy as jnp
from jax import lax
from jax.experimental import pallas as pl
from jax.experimental.pallas import tpu as pltpu
from jax.sharding import PartitionSpec as P

taper_reach = 0.6
tile_side = 128
f32, bf16 = jnp.float32, jnp.bfloat16
anywhere = pl.BlockSpec(memory_space=pl.ANY)
in_vmem = pl.BlockSpec(memory_space=pltpu.VMEM)
span_edges = (0, 6, 8)
small_cost = pl.CostEstimate(flops=1000, bytes_accessed=1000, transcendentals=0)
vmem_limit = 56 * 1024 * 1024


def dot(a, b):
    return lax.dot_general(a, b, (((1,), (0,)), ((), ())), preferred_element_type=f32)


def split(x):
    high = x.astype(bf16)
    return high, (x - high.astype(f32)).astype(bf16)


def swap(x, axis, distance):
    size = lax.axis_size(axis)
    return lax.ppermute(x, axis, [(i, i ^ distance) for i in range(size)])


def after(x, *deps):
    return lax.optimization_barrier((x, *deps))[0] if deps else x


def join_kernel(*refs):
    out_ref, sem = refs[-2:]
    at = 0
    for ref in refs[:-2]:
        size = ref.shape[0]
        pltpu.make_async_copy(ref, out_ref.at[pl.ds(at, size)], sem).start()
        at += size
    pltpu.make_async_copy(out_ref, out_ref, sem).wait()


def join(*blocks):
    count = sum(block.shape[0] for block in blocks)
    return pl.pallas_call(
        join_kernel,
        out_shape=jax.ShapeDtypeStruct((count, *blocks[0].shape[1:]), f32),
        in_specs=[anywhere] * len(blocks),
        out_specs=in_vmem,
        scratch_shapes=[pltpu.SemaphoreType.DMA],
        compiler_params=pltpu.CompilerParams(vmem_limit_bytes=vmem_limit),
        cost_estimate=small_cost,
    )(*blocks)


def prep_obs_kernel(order, near_ref, far_ref, high_ref, low_ref):
    blocks, rows, width = near_ref.shape
    refs = [near_ref.at[i] for i in range(blocks)] + [far_ref.at[i] for i in range(blocks)]
    total = jnp.zeros((1, width), f32)
    for ref in refs:
        total += jnp.sum(ref[...], axis=0, keepdims=True)
    mean = total / (2 * blocks * rows)
    for i, ref in enumerate(refs):
        high, low = split((ref[...] - mean).T)
        at = pl.ds(order[i] * rows, rows)
        high_ref[:, at] = high
        low_ref[:, at] = low


def prep_obs(pair, order):
    blocks, rows, width = pair[0].shape
    band = 256 if width % 256 == 0 else 128
    whole = pl.BlockSpec((blocks, rows, band), lambda j: (0, 0, j))
    return pl.pallas_call(
        functools.partial(prep_obs_kernel, order),
        grid=(width // band,),
        out_shape=[jax.ShapeDtypeStruct((width, 2 * blocks * rows), bf16)] * 2,
        in_specs=[whole] * 2,
        out_specs=[pl.BlockSpec((band, 2 * blocks * rows), lambda j: (j, 0))] * 2,
        compiler_params=pltpu.CompilerParams(vmem_limit_bytes=vmem_limit),
        cost_estimate=small_cost,
    )(*pair)


def update_kernel(parts, order, first, start, *refs):
    me_ref, points, refs = refs[0], refs[1], refs[2:]
    me = me_ref[0]
    nobs = len(parts)
    obs_high, refs = refs[:nobs], refs[nobs:]
    obs_low, refs = refs[:nobs], refs[nobs:]
    ninn = len(refs) - (15 if first else 16)
    inn, refs = refs[:ninn], refs[ninn:]
    taper = refs[0]
    refs = refs[1 if first else 2 :]
    out, total, x_high, x_low, yh, yl, w, tap, kh, kl, sem_x, sem_y, sem_w, sem_out = refs
    members, width = total.shape
    local = len(order)
    ml = members // local
    window = tap.shape[0]
    slot_obs = window // 3
    band = min(512, members)
    x_copies = []
    for r in range(local):
        paired = len(points.shape) == 4
        block = points.at[lax.div(me ^ r, 2), r % 2] if paired else points.at[me ^ r]
        x_copies.append(pltpu.make_async_copy(block, total.at[pl.ds(r * ml, ml)], sem_x.at[r]))
    y_copies = []
    for i, (slot, at, size) in enumerate(parts):
        here = pl.ds(at, size)
        y_copies.append(
            [
                pltpu.make_async_copy(obs_high[i], yh.at[here], sem_y.at[slot, 0]),
                pltpu.make_async_copy(obs_low[i], yl.at[here], sem_y.at[slot, 1]),
                pltpu.make_async_copy(
                    taper.at[here, pl.ds(start, width)], tap.at[here], sem_y.at[slot, 2]
                ),
            ]
        )
    w_copies = []
    for i in range(ninn):
        slot, part = i // 2, i % 2
        here = pl.ds(slot * slot_obs, slot_obs)
        for k in range(local // 2):
            at = pl.ds(order[part * (local // 2) + k] * ml, ml)
            w_copies.append(pltpu.make_async_copy(inn[i].at[k], w.at[at, here], sem_w))
    for copy in x_copies + y_copies[0]:
        copy.start()
    for r, copy in enumerate(x_copies):
        copy.wait()
        at = pl.ds(r * ml, ml)
        x_high[at, :], x_low[at, :] = split(total[at, :])
    for copy in y_copies[1] + y_copies[2] + w_copies:
        copy.start()

    def weights(slot, carry):
        here = pl.ds(pl.multiple_of(slot * slot_obs, 128), slot_obs)
        pltpu.make_async_copy(yh.at[here], yh.at[here], sem_y.at[slot, 0]).wait()
        pltpu.make_async_copy(yl.at[here], yl.at[here], sem_y.at[slot, 1]).wait()
        pltpu.make_async_copy(tap.at[here], tap.at[here], sem_y.at[slot, 2]).wait()
        cov = dot(yh[here, :], x_high[...]) + dot(yl[here, :], x_high[...])
        cov += dot(yh[here, :], x_low[...])
        kh[here, :], kl[here, :] = split(cov * tap[here, :])
        return carry

    lax.fori_loop(0, 3, weights, 0)
    pltpu.make_async_copy(w, w, sem_w).wait()
    blocks = band // ml

    def change(i, carry):
        at = pl.ds(pl.multiple_of(i * band, band), band)
        w_high, w_low = split(w[at, :])
        total[at, :] += dot(w_high, kh[...]) + dot(w_low, kh[...]) + dot(w_high, kl[...])
        for r in range(blocks):
            block = i * blocks + r
            pltpu.make_async_copy(
                total.at[pl.ds(pl.multiple_of(block * ml, ml), ml)],
                out.at[pl.ds(pl.multiple_of((me ^ block) * ml, ml), ml), pl.ds(start, width)],
                sem_out.at[block],
            ).start()
        return carry

    lax.fori_loop(0, members // band, change, 0)
    for block in range(local):
        pltpu.make_async_copy(
            total.at[pl.ds(block * ml, ml)],
            out.at[pl.ds(pl.multiple_of((me ^ block) * ml, ml), ml), pl.ds(start, width)],
            sem_out.at[block],
        ).wait()


def side_copies(side, state_ref, begin, out_refs, sem):
    width = out_refs[0].shape[1]
    per_device = state_ref.shape[1] // (2 * len(out_refs))
    copies = []
    for z, out_ref in enumerate(out_refs):
        at = pl.multiple_of((2 * z + side) * per_device + begin, 128)
        copies.append(pltpu.make_async_copy(state_ref.at[:, pl.ds(at, width)], out_ref, sem))
    return copies


def given_kernel(begin, side_ref, state_ref, out_ref, sem):
    refs = [out_ref.at[z] for z in range(out_ref.shape[0])]
    for copy in side_copies(1 - side_ref[0], state_ref, begin, refs, sem):
        copy.start()
    pltpu.make_async_copy(out_ref, out_ref, sem).wait()


def given(side, state, groups, begin, width):
    return pl.pallas_call(
        functools.partial(given_kernel, begin),
        out_shape=jax.ShapeDtypeStruct((groups // 2, state.shape[0], width), f32),
        in_specs=[pl.BlockSpec(memory_space=pltpu.SMEM), anywhere],
        out_specs=in_vmem,
        scratch_shapes=[pltpu.SemaphoreType.DMA],
        compiler_params=pltpu.CompilerParams(vmem_limit_bytes=vmem_limit),
        cost_estimate=small_cost,
    )(side, state)


def regroup_kernel(begin, state_ref, out_ref, sem):
    groups, ml, width = out_ref.shape
    per_device = state_ref.shape[1] // groups
    for g in range(groups):
        here = pl.ds(g * per_device + begin, width)
        pltpu.make_async_copy(state_ref.at[:, here], out_ref.at[g], sem).start()
    pltpu.make_async_copy(out_ref, out_ref, sem).wait()


def regroup(state, groups, begin, width):
    return pl.pallas_call(
        functools.partial(regroup_kernel, begin),
        out_shape=jax.ShapeDtypeStruct((groups, state.shape[0], width), f32),
        in_specs=[anywhere],
        out_specs=in_vmem,
        scratch_shapes=[pltpu.SemaphoreType.DMA],
        compiler_params=pltpu.CompilerParams(vmem_limit_bytes=vmem_limit),
        cost_estimate=small_cost,
    )(state)


def kept_kernel(begin, side_ref, state_ref, out_ref, held, sem_in, sem_out):
    blocks = held.shape[0]
    refs = [held.at[z] for z in range(blocks)]
    for copy in side_copies(side_ref[0], state_ref, begin, refs, sem_in):
        copy.start()
    pltpu.make_async_copy(held, held, sem_in).wait()
    for z in range(blocks):
        pltpu.make_async_copy(held.at[z], out_ref.at[z, 0], sem_out).start()
    pltpu.make_async_copy(held, held, sem_out).wait()


def kept(side, state, groups, begin, width):
    blocks, ml = groups // 2, state.shape[0]
    return pl.pallas_call(
        functools.partial(kept_kernel, begin),
        out_shape=jax.ShapeDtypeStruct((blocks, 2, ml, width), f32),
        in_specs=[pl.BlockSpec(memory_space=pltpu.SMEM), anywhere],
        out_specs=anywhere,
        scratch_shapes=[
            pltpu.VMEM((blocks, ml, width), f32),
            pltpu.SemaphoreType.DMA,
            pltpu.SemaphoreType.DMA,
        ],
        compiler_params=pltpu.CompilerParams(vmem_limit_bytes=vmem_limit),
        cost_estimate=small_cost,
    )(side, state)


def filled_kernel(got_ref, old_ref, out_ref, held, sem_in, sem_out):
    pltpu.make_async_copy(got_ref, held, sem_in).start()
    pltpu.make_async_copy(held, held, sem_in).wait()
    for z in range(held.shape[0]):
        pltpu.make_async_copy(held.at[z], out_ref.at[z, 1], sem_out).start()
    pltpu.make_async_copy(held, held, sem_out).wait()


def filled(got, old):
    return pl.pallas_call(
        filled_kernel,
        out_shape=jax.ShapeDtypeStruct(old.shape, f32),
        in_specs=[anywhere, anywhere],
        out_specs=anywhere,
        scratch_shapes=[
            pltpu.VMEM(got.shape, f32),
            pltpu.SemaphoreType.DMA,
            pltpu.SemaphoreType.DMA,
        ],
        input_output_aliases={1: 0},
        compiler_params=pltpu.CompilerParams(vmem_limit_bytes=vmem_limit),
        cost_estimate=small_cost,
    )(got, old)


def update(me, points, obs, parts, innov, order, taper, out, start, per_device):
    width = points.shape[-1]
    members = points.size // width
    window_obs = taper.shape[0]
    first = out is None
    operands = [me, points, *[o[0] for o in obs], *[o[1] for o in obs], *innov, taper]
    operands += [] if first else [out]
    return pl.pallas_call(
        functools.partial(update_kernel, parts, order, first, start),
        out_shape=jax.ShapeDtypeStruct((members, per_device), f32),
        in_specs=[pl.BlockSpec(memory_space=pltpu.SMEM)] + [anywhere] * (len(operands) - 1),
        out_specs=anywhere,
        scratch_shapes=[
            pltpu.VMEM((members, width), f32),
            pltpu.VMEM((members, width), bf16),
            pltpu.VMEM((members, width), bf16),
            pltpu.VMEM((window_obs, members), bf16),
            pltpu.VMEM((window_obs, members), bf16),
            pltpu.VMEM((members, window_obs), f32),
            pltpu.VMEM((window_obs, width), f32),
            pltpu.VMEM((window_obs, width), bf16),
            pltpu.VMEM((window_obs, width), bf16),
            pltpu.SemaphoreType.DMA((len(order),)),
            pltpu.SemaphoreType.DMA((3, 3)),
            pltpu.SemaphoreType.DMA,
            pltpu.SemaphoreType.DMA((len(order),)),
        ],
        input_output_aliases={} if first else {len(operands) - 1: 0},
        compiler_params=pltpu.CompilerParams(vmem_limit_bytes=vmem_limit),
        cost_estimate=small_cost,
    )(*operands)


def shards(state, obs_ensemble, innovations, obs_coords, tile_list, tile_counts):
    ml = state.shape[0]
    groups = lax.axis_size("mem")
    domains = lax.axis_size("dom")
    per_domain = state.shape[1]
    per_device = per_domain // groups
    obs_local = obs_ensemble.shape[1]
    members = ml * groups
    me = lax.axis_index("mem")
    domain = lax.axis_index("dom")
    odd = domain % 2

    bits = []
    b = groups // 2
    while b >= 1:
        bits.append(b)
        b //= 2
    order = [0]
    for b in bits:
        order = order + [r ^ b for r in order]

    across = [((i + 1) % domains, (i + 2) % domains) for i in range(0, domains, 2)]
    across = across + [(t, s) for s, t in across]
    chip = [(i, i ^ 1) for i in range(domains)]

    def tapered(coord_beside, coord_beyond):
        position = jnp.stack([jnp.int32(1), 2 - 2 * odd, 2 * odd]).astype(jnp.int32)
        coords = jnp.concatenate([obs_coords, coord_beside, coord_beyond], axis=1)
        nblocks = per_device // tile_side
        window = obs_local // tile_side
        point_ids, obs_ids = tile_list[0, 0, 0], tile_list[0, 0, 1]
        slots = point_ids.shape[0]
        live = (jnp.arange(slots, dtype=jnp.int32) < tile_counts[0, 0]).astype(f32)
        block_ids = (position[:, None] * window + jnp.arange(window, dtype=jnp.int32)[None]).reshape(-1)
        by_obs = (obs_ids[None, :] == block_ids[:, None]).astype(f32) * live[None]
        by_point = (point_ids[:, None] == jnp.arange(nblocks, dtype=jnp.int32)[None]).astype(f32)
        mask = jnp.sum(by_obs[:, :, None] * by_point[None], axis=1)
        mask = jnp.repeat(mask, tile_side, axis=1) / (members - 1)
        within = me * per_device + jnp.arange(per_device, dtype=jnp.int32)
        point_x = domain.astype(f32) + ((within % 32).astype(f32) + 0.5) / 32.0
        point_y = ((within // 32).astype(f32) + 0.5) / float(per_domain // 32)
        gap_x = jnp.abs(point_x[None, :] - coords[0][:, None])
        gap_x = jnp.minimum(gap_x, float(domains) - gap_x)
        gap_y = point_y[None, :] - coords[1][:, None]
        taper = jnp.exp(-(gap_x * gap_x + gap_y * gap_y) / (2.0 * taper_reach * taper_reach))
        taper = (taper.reshape(-1, tile_side, per_device) * mask[:, None, :]).reshape(-1, per_device)
        return taper

    edges = [per_device * e // 8 for e in span_edges]
    spans = [(edges[c], edges[c + 1] - edges[c]) for c in range(len(edges) - 1)]
    sides = [[i for i in range(groups) if i % 2 == s] for s in range(2)]
    my_side = (me % 2).astype(jnp.int32).reshape(1)

    def assembled(blocks, within, *deps):
        return lax.all_to_all(
            after(blocks, *deps),
            "mem",
            split_axis=0,
            concat_axis=0,
            tiled=True,
            axis_index_groups=within,
        )

    def far_gathered(x, ahead, *deps):
        own, others, got = after(x[None], *deps), [], []
        early = swap(own if ahead is None else after(own, ahead), "mem", bits[-2])
        for b in bits[:-2]:
            got.append(swap(join(own, *others) if others else own, "mem", b))
            others.append(got[-1])
        got.append(swap(join(*others) if len(others) > 1 else others[0], "mem", bits[-2]))
        return join(own, *others, early, got[-1]), got

    def cross(x, *deps):
        return lax.ppermute(after(x, *deps), "dom", across)

    def beside(x, *deps):
        return lax.ppermute(after(x, *deps), "dom", chip)

    def side(x, *deps):
        return swap(after(x, *deps), "mem", 1)

    give = given(my_side, state, groups, *spans[0])
    first = side(give)
    obs_near, obs_got = far_gathered(obs_ensemble, give)
    inn_near, inn_got = far_gathered(innovations, None, obs_got[0])
    coord_beside = beside(obs_coords, obs_got[0])
    coord_beyond = cross(obs_coords, obs_got[0])
    taper = tapered(coord_beside, coord_beyond)
    obs_near_beyond = cross(obs_near, coord_beyond, coord_beside)
    obs_far = side(obs_near)
    paired = filled(first, kept(my_side, state, groups, *spans[0]))
    points = [assembled(paired, sides, obs_got[-1], inn_got[-1])]
    obs_near_beside = beside(obs_near, obs_near_beyond, obs_far, taper, inn_near)
    pause = beside(obs_far, obs_near_beside)
    inn_near_beyond = cross(inn_near, pause)
    inn_far = side(inn_near, pause)
    obs_far_beside = pause
    ready_own = prep_obs((obs_near, obs_far), order)
    ready_beside = prep_obs((obs_near_beside, obs_far_beside), order)
    blocks = regroup(after(state, obs_got[-1]), groups, *spans[1])
    obs_far_beyond = cross(obs_far, inn_near_beyond, inn_far, obs_far_beside, ready_own[0], blocks)
    inn_far_beyond = side(inn_near_beyond, inn_far)
    inn_near_beside = beside(inn_near, obs_far_beyond, inn_far_beyond, ready_beside[0])
    inn_far_beside = beside(inn_far, inn_near_beside)
    points.append(assembled(blocks, None, points[0]))
    ready_beyond = prep_obs((obs_near_beyond, obs_far_beyond), order)
    obs = [ready_own, ready_beside, ready_beyond]
    innov = [inn_near, inn_far, inn_near_beside, inn_far_beside, inn_near_beyond, inn_far_beyond]
    parts = [(slot, slot * obs_local, obs_local) for slot in range(3)]
    out = None
    for c in range(len(spans)):
        out = update(
            me.astype(jnp.int32).reshape(1),
            points[c],
            obs,
            parts,
            innov,
            order,
            taper,
            out,
            spans[c][0],
            per_device,
        )
    return out


def solution(mesh):
    return jax.shard_map(
        shards,
        mesh=mesh,
        in_specs=(
            P("mem", "dom"),
            P("mem", "dom"),
            P("mem", "dom"),
            P(None, "dom"),
            P("dom", "mem", None, None),
            P("dom", "mem"),
        ),
        out_specs=P(None, ("dom", "mem")),
        check_vma=False,
    )
```
